512 devices in a mesh: dp: 8 (over y), row: 16 (over z, x_hi), lon: 4 (over x_lo, core).
Axes of the slice: x: 4 (x_hi: 2, x_lo: 2; x = x_hi * 2 + x_lo), y: 8, z: 8, core: 2. Of those that a mesh axis runs over, the one named last changes fastest.
Arguments:
- features: bfloat16 [8, 96, 144, 2048], P('dp', 'row', 'lon'), may hold values from -6 to 6
- depthwise_kernels: bfloat16 [2, 3, 3, 2048], replicated, may hold values from -2 to 2
- point_weights: bfloat16 [2, 2048, 256], replicated, may hold values from -0.125 to 0.125
- proj_weight: bfloat16 [512, 256], replicated, may hold values from -0.25 to 0.25
- class_weight: bfloat16 [256, 3], replicated, may hold values from -1.25 to 1.25
- labels: int32 [8, 96, 144], P('dp', 'row', 'lon'), may hold values from 0 to 2
Outputs:
- input_grad: bfloat16 [8, 96, 144, 2048], P('dp', 'row', 'lon')
- point_grad: float32 [2, 2048, 256], P(None, ('row', 'lon'), 'dp')
The draws below stay inside these ranges and needn't reach their ends.
All inputs are finite; a program needn't handle non-finite values.
Results may differ from the reference program's by a relative error of at most 0.025.
Values may be sent and summed in bfloat16 or wider, within the bound.
A program may use at most 128 MiB of HBM per device.

```python
import math
import jax
import jax.numpy as jnp
from jax import lax

C = 2048
OUTC = 256
CLASSES = 3
BRANCHES = 2
DILATION_INNER = 12
DILATION_OUTER = 36
IMAGES = 8
H = 96
W = 144


def place_ends(values, own_key, smallest, top_value):
    spot = [jax.random.randint(jax.random.fold_in(own_key, axis), (), 0, length) for axis, length in enumerate(values.shape)]
    main_axis = values.shape.index(max(values.shape))
    next_to = spot[:main_axis] + [(spot[main_axis] + 1) % values.shape[main_axis]] + spot[main_axis + 1:]
    return values.at[tuple(spot)].set(smallest).at[tuple(next_to)].set(top_value)


def steps_of(key, shape, shards, low, top_value):
    def one(axis_at, blocks):
        steps = jax.random.uniform(jax.random.fold_in(jax.random.fold_in(key, 6), axis_at), (blocks,), jnp.float32, low / len(shards), top_value / len(shards))
        return jnp.repeat(jnp.exp(steps), shape[axis_at] // blocks).reshape((-1,) + (1,) * (len(shape) - axis_at - 1))

    gain = one(*shards[0])
    for cut in shards[1:]:
        gain = gain * one(*cut)
    return gain


def centred(rng, dims, spread, limit, cuts=(), kind=jnp.bfloat16):
    entries = jax.random.normal(rng, dims, jnp.float32) * spread
    if len(cuts) > 0:
        entries = steps_of(rng, dims, cuts, -0.22, 0.18) * entries
    return jnp.clip(entries, min=-limit, max=limit).astype(kind)


def setup_inputs(seed: int = 0) -> dict:
    splits = jax.random.split(jax.random.key(seed), 7)
    features = centred(splits[0], (IMAGES, H, W, C), 1.0, 6.0, ((0, 8), (1, 16), (2, 4)))
    depthwise_kernels = centred(splits[1], (BRANCHES, 3, 3, C), 0.35, 2.0)
    point_weights = centred(splits[2], (BRANCHES, C, OUTC), C ** -0.5, 0.125)
    proj_weight = centred(splits[3], (BRANCHES * OUTC, OUTC), (BRANCHES * OUTC) ** -0.5, 0.25)
    class_weight = centred(splits[4], (OUTC, CLASSES), 0.2, 1.25)
    labels = place_ends(jax.random.randint(splits[5], (IMAGES, H, W), 0, CLASSES), jax.random.fold_in(splits[5], 1), 0, CLASSES - 1).astype(jnp.int32)
    return {"features": features, "depthwise_kernels": depthwise_kernels, "point_weights": point_weights, "proj_weight": proj_weight, "class_weight": class_weight, "labels": labels}


loss_scale = 32.0

def silu_slope(value):
    sigma = jax.nn.sigmoid(value)
    return sigma * (1.0 + value * (1.0 - sigma))

def partial_rows(image_map, kernel, dilation, direction):
    partials = []
    for row_tap in range(3):
        total_sum = jnp.zeros(image_map.shape, jnp.float32)
        for col_tap in range(3):
            rolled = jnp.roll(image_map, -direction * (col_tap - 1) * dilation, axis=1)
            total_sum = total_sum + rolled.astype(jnp.float32) * kernel[row_tap, col_tap].astype(jnp.float32)
        partials.append(total_sum.astype(jnp.bfloat16))
    return partials

def combine_rows(partials, dilation, direction):
    height = partials[0].shape[0]
    total_sum = partials[1].astype(jnp.float32)
    for row_tap in (0, 2):
        offset = direction * (row_tap - 1)
        padded = jnp.pad(partials[row_tap], ((dilation, dilation), (0, 0), (0, 0)))
        begin_row = dilation + offset * dilation
        total_sum = total_sum + padded[begin_row:begin_row + height].astype(jnp.float32)
    return total_sum

def one_image(image_map, label_map, depthwise_kernels, point_weights, proj_weight, class_weight):
    dilation_list = (DILATION_INNER, DILATION_OUTER)
    height, wide_cols, channels = image_map.shape
    pixels = height * wide_cols
    flat_depth = []
    for branch_index in range(2):
        depth = combine_rows(partial_rows(image_map, depthwise_kernels[branch_index], dilation_list[branch_index], 1), dilation_list[branch_index], 1)
        flat_depth.append(depth.astype(jnp.bfloat16).reshape(pixels, channels))
    point_pre = [jnp.dot(flat_depth[branch_index], point_weights[branch_index], preferred_element_type=jnp.float32) for branch_index in range(2)]
    joined = jnp.concatenate([jax.nn.silu(point_pre[branch_index]).astype(jnp.bfloat16) for branch_index in range(2)], axis=1)
    proj_pre = jnp.dot(joined, proj_weight, preferred_element_type=jnp.float32)
    projected = jax.nn.silu(proj_pre).astype(jnp.bfloat16)
    logits = jnp.dot(projected, class_weight, preferred_element_type=jnp.float32)
    label_flat = label_map.reshape(pixels)
    onehot = (label_flat[:, None] == jnp.arange(CLASSES, dtype=jnp.int32)[None, :]).astype(jnp.float32)
    grad_logits = (loss_scale * (jax.nn.softmax(logits, axis=1) - onehot)).astype(jnp.bfloat16)
    grad_proj = (jnp.dot(grad_logits, class_weight.T, preferred_element_type=jnp.float32) * silu_slope(proj_pre)).astype(jnp.bfloat16)
    grad_joined = jnp.dot(grad_proj, proj_weight.T, preferred_element_type=jnp.float32)
    point_terms = []
    input_total = jnp.zeros(image_map.shape, jnp.float32)
    out_width = point_weights.shape[2]
    for branch_index in range(2):
        grad_act = (grad_joined[:, branch_index * out_width:(branch_index + 1) * out_width] * silu_slope(point_pre[branch_index])).astype(jnp.bfloat16)
        point_terms.append(jnp.dot(flat_depth[branch_index].T, grad_act, preferred_element_type=jnp.float32))
        grad_depth = jnp.dot(grad_act, point_weights[branch_index].T, preferred_element_type=jnp.float32).astype(jnp.bfloat16)
        grad_depth = grad_depth.reshape(height, wide_cols, channels)
        back_parts = partial_rows(grad_depth, depthwise_kernels[branch_index], dilation_list[branch_index], -1)
        input_total = input_total + combine_rows(back_parts, dilation_list[branch_index], -1)
    return (input_total.astype(jnp.bfloat16), jnp.stack(point_terms))

def reference(features, depthwise_kernels, point_weights, proj_weight, class_weight, labels):

    def per_image(image_pair):
        return one_image(image_pair[0], image_pair[1], depthwise_kernels, point_weights, proj_weight, class_weight)
    results = lax.map(per_image, (features, labels))
    pixel_count = features.shape[0] * features.shape[1] * features.shape[2]
    grad_scale = 1.0 / math.sqrt(pixel_count)
    point_grad = lax.optimization_barrier(jnp.sum(results[1], axis=0)) * grad_scale
    return (results[0], point_grad)
```

```python
import functools
import math

import jax
import jax.numpy as jnp
from jax import lax
from jax.experimental import pallas as pl
from jax.experimental.pallas import tpu as pltpu
from jax.sharding import PartitionSpec as P

DILATION_INNER = 12
DILATION_OUTER = 36
GROUP = DILATION_INNER
LOSS_SCALE = 32.0
MESH = pl.DeviceIdType.MESH
NN = (((1,), (0,)), ((), ()))
NT = (((1,), (1,)), ((), ()))
F32 = jnp.float32
BF16 = jnp.bfloat16


def dot(a, b, dims=NN):
    return lax.dot_general(a, b, dims, preferred_element_type=F32)


def slope(value, sigma):
    return sigma * (1.0 + value * (1.0 - sigma))


def kernel(
    size, hops, scale,
    x_ref, k_ref, pw_ref, proj_ref, cls_ref, lab_ref,
    ig_ref, pg_ref,
    kf_ref, kb_ref, cacc_ref,
    yso_ref, yro_ref, ysi_ref, yri_ref,
    cs_ref, cr_ref,
    g0_ref, g1_ref, gt_ref, igacc_ref,
    t_ref, rc_ref, s_ref, ry_ref, u0_ref, rz0_ref, rz1_ref, u1_ref, ry1_ref, v_ref, rx_ref,
    ss_y, rs_y, ss_c, rs_c, ss_gz, rs_gz, ss_gl, rs_gl,
    ss_core, rs_core, ss_ry, rs_ry, ss_rz, rs_rz, ss_rx, rs_rx,
):
    ndp, nrow, nlon = size
    nz = nrow // 2
    channels = x_ref.shape[1]
    outc = pw_ref.shape[2]
    gp = g0_ref.shape[2]
    pix = 3 * gp
    pix_pad = x_ref.shape[0]
    y = lax.axis_index("dp")
    row = lax.axis_index("row")
    lon = lax.axis_index("lon")
    z = row // 2
    xh = row % 2
    core = lon % 2
    member = xh * nlon + lon
    right = {"lon": (lon + 1) % nlon}
    left = {"lon": (lon + nlon - 1) % nlon}
    partner = {"lon": lon + 1 - 2 * core}

    def along(shift):
        return {"row": (row + shift + nrow) % nrow}

    def dp_peer(k):
        return (y + k) % ndp

    def z_peer(k):
        return (z + k) % nz

    def x_peer(k):
        other = (member + k) % (2 * nlon)
        return {"row": z * 2 + other // nlon, "lon": other % nlon}

    started = []

    def send(src, dst, ssem, rsem, device):
        copy = pltpu.make_async_remote_copy(
            src_ref=src, dst_ref=dst, send_sem=ssem, recv_sem=rsem,
            device_id=device, device_id_type=MESH,
        )
        copy.start()
        started.append(copy)
        return copy

    barrier = pltpu.get_barrier_semaphore()
    peers = [left, right]
    for shift in hops:
        peers += [along(shift), along(-shift)]
    peers += [{"dp": dp_peer(k)} for k in range(1, ndp)]
    peers += [{"row": z_peer(k) * 2 + xh} for k in range(1, nz)]
    peers += [x_peer(k) for k in range(1, 2 * nlon)]
    for peer in peers:
        pl.semaphore_signal(barrier, inc=1, device_id=peer, device_id_type=MESH)

    kf_ref[...] = k_ref[...].astype(F32)
    for t in range(18):
        kb_ref[t] = jnp.broadcast_to(kf_ref[t : t + 1, :], (16, channels)).astype(BF16)

    def taps(b, i):
        x = x_ref[:pix, :].reshape(pix // 16, 16, channels)
        out = []
        for j in (0, 2, 1):
            scaled = (x * kb_ref[b * 9 + i * 3 + j][None]).reshape(pix, channels)
            out.append(dot(scaled, pw_ref[b]))
        return out

    pl.semaphore_wait(barrier, len(peers))

    lon_copies = {}

    def outer_taps(i):
        y0, y2, y1 = taps(1, i)
        cacc_ref[3 + i] = y1
        yso_ref[i, 0] = y0.astype(BF16)
        yso_ref[i, 1] = y2.astype(BF16)
        lon_copies[1, i] = [
            send(yso_ref.at[i, 0], yro_ref.at[i, 0], ss_y.at[6 + 2 * i], rs_y.at[6 + 2 * i], right),
            send(yso_ref.at[i, 1], yro_ref.at[i, 1], ss_y.at[7 + 2 * i], rs_y.at[7 + 2 * i], left),
        ]

    def inner_taps(i):
        y0, y2, y1 = taps(0, i)
        ysi_ref[i, 0] = y0[2 * gp :].astype(BF16)
        ysi_ref[i, 1] = y2[:gp].astype(BF16)
        lon_copies[0, i] = [
            send(ysi_ref.at[i, 0], yri_ref.at[i, 0], ss_y.at[2 * i], rs_y.at[2 * i], right),
            send(ysi_ref.at[i, 1], yri_ref.at[i, 1], ss_y.at[2 * i + 1], rs_y.at[2 * i + 1], left),
        ]
        cacc_ref[i] = y1
        cacc_ref[i, gp:, :] += y0[: 2 * gp]
        cacc_ref[i, : 2 * gp, :] += y2[gp:]

    def columns_done(b, i):
        for copy in lon_copies[b, i]:
            copy.wait_recv()
        if b == 1:
            cacc_ref[3 + i] += yro_ref[i, 0].astype(F32) + yro_ref[i, 1].astype(F32)
        else:
            cacc_ref[i, :gp, :] += yri_ref[i, 0].astype(F32)
            cacc_ref[i, 2 * gp :, :] += yri_ref[i, 1].astype(F32)

    row_copies = {}

    def rows_out(b, i):
        columns_done(b, i)
        half = i // 2
        n = 2 * b + half
        cs_ref[n] = cacc_ref[3 * b + i].astype(BF16)
        row_copies[b, i] = send(
            cs_ref.at[n], cr_ref.at[n], ss_c.at[n], rs_c.at[n], along(hops[b] * (1 - i))
        )

    outer_taps(0)
    outer_taps(2)
    inner_taps(0)
    rows_out(1, 0)
    inner_taps(2)
    rows_out(1, 2)
    outer_taps(1)
    rows_out(0, 0)
    rows_out(0, 2)
    inner_taps(1)
    columns_done(0, 1)
    columns_done(1, 1)

    def inside(b, i):
        source = row + hops[b] * (i - 1)
        return jnp.logical_and(source >= 0, source < nrow)

    point_pre = []
    for b in (0, 1):
        total = cacc_ref[3 * b + 1]
        for i in (0, 2):
            row_copies[b, i].wait_recv()
            total = total + jnp.where(inside(b, i), cr_ref[2 * b + i // 2].astype(F32), 0.0)
        point_pre.append(total)

    sig = [jax.nn.sigmoid(v) for v in point_pre]
    joined = jnp.concatenate([(v * s).astype(BF16) for v, s in zip(point_pre, sig)], axis=1)
    proj_pre = dot(joined, proj_ref[...])
    proj_sig = jax.nn.sigmoid(proj_pre)
    projected = (proj_pre * proj_sig).astype(BF16)
    logits = dot(projected, cls_ref[...])
    lane = lax.broadcasted_iota(jnp.int32, logits.shape, 1)
    real = lane < 3
    top = jnp.max(jnp.where(real, logits, -jnp.inf), axis=1, keepdims=True)
    power = jnp.where(real, jnp.exp(jnp.where(real, logits - top, 0.0)), 0.0)
    soft = power / jnp.sum(power, axis=1, keepdims=True)
    onehot = (lane == lab_ref[...]).astype(F32)
    grad_logits = (LOSS_SCALE * (soft - onehot)).astype(BF16)
    grad_proj = (dot(grad_logits, cls_ref[...], NT) * slope(proj_pre, proj_sig)).astype(BF16)
    grad_joined = dot(grad_proj, proj_ref[...], NT)
    grad_act = [
        (grad_joined[:, b * outc : (b + 1) * outc] * slope(point_pre[b], sig[b])).astype(BF16)
        for b in (0, 1)
    ]
    g0_ref[1, 1:4] = grad_act[0].reshape(3, gp, outc)
    g1_ref[1, 3:6] = grad_act[1].reshape(3, gp, outc)

    z_copies = {}
    g_copies = {}
    refs = (g0_ref, g1_ref)

    def rows_back(b, i):
        own = slice(1, 4) if b == 0 else slice(3, 6)
        n = 2 * b + i // 2
        z_copies[b, i] = send(
            refs[b].at[1, own], refs[b].at[i, own], ss_gz.at[n], rs_gz.at[n],
            along(hops[b] * (i - 1)),
        )

    def columns_back(b, i):
        n = 2 * (3 * b + i)
        if b == 0:
            ends = ((slice(3, 4), slice(0, 1), right), (slice(1, 2), slice(4, 5), left))
        else:
            ends = ((slice(3, 6), slice(0, 3), right), (slice(3, 6), slice(6, 9), left))
        g_copies[b, i] = [
            send(refs[b].at[i, src], refs[b].at[i, dst], ss_gl.at[n + e], rs_gl.at[n + e], device)
            for e, (src, dst, device) in enumerate(ends)
        ]

    for b in (0, 1):
        for i in (0, 2):
            rows_back(b, i)
    columns_back(0, 1)
    columns_back(1, 1)
    for i in (0, 2):
        z_copies[0, i].wait_recv()
        columns_back(0, i)

    for b in (0, 1):
        for i in (0, 2):
            first = b * 9 + i * 3
            source = row - hops[b] * (i - 1)
            keep = jnp.logical_and(source >= 0, source < nrow).astype(F32)
            kf_ref[first : first + 3, :] = kf_ref[first : first + 3, :] * keep

    def window(b, i, j):
        start = 2 - j if b == 0 else 3 * (2 - j)
        return refs[b][i, start : start + 3].reshape(pix, outc)

    tile = 256
    tiles = channels // tile
    chunk = outc // ndp
    half_rows = chunk // 2

    def turned(b, i):
        for j in range(3):
            block = window(b, i, j).astype(F32)
            block = jnp.concatenate([block, jnp.zeros((pix_pad - pix, outc), F32)], axis=0)
            gt_ref[3 * i + j] = block.T.astype(BF16)

    def point_terms(b):
        def step(n, carry):
            cols = pl.ds(pl.multiple_of(n * tile, tile), tile)
            terms = dot(gt_ref[...].reshape(9 * outc, pix_pad), x_ref[:, cols])
            total = None
            for t in range(9):
                term = terms[t * outc : (t + 1) * outc] * kf_ref[b * 9 + t : b * 9 + t + 1, cols]
                total = term if total is None else total + term
            t_ref[b, :, :, :, cols] = total.astype(BF16).reshape(ndp, 2, half_rows, tile)
            return carry

        lax.fori_loop(0, tiles, step, 0)

    def input_terms(b):
        def step(n, carry):
            cols = pl.ds(pl.multiple_of(n * tile, tile), tile)
            weights = pw_ref[b, cols, :]
            total = None
            for i in range(3):
                if b == 0:
                    spread = dot(g0_ref[i].reshape(5 * gp, outc), weights, NT)
                else:
                    spread = dot(g1_ref[i].reshape(9 * gp, outc), weights, NT)
                for j in range(3):
                    start = (2 - j) * gp if b == 0 else (2 - j) * pix
                    t = b * 9 + 3 * i + j
                    term = spread[start : start + pix] * kf_ref[t : t + 1, cols]
                    total = term if total is None else total + term
            if b == 0:
                igacc_ref[:, cols] = total
            else:
                ig_ref[:, cols] = (igacc_ref[:, cols] + total).astype(BF16)
            return carry

        lax.fori_loop(0, tiles, step, 0)

    def core_out(b):
        return send(
            t_ref.at[b, :, 1 - core], rc_ref.at[b], ss_core.at[b], rs_core.at[b], partner
        )

    def core_in(b, copy):
        copy.wait_recv()
        s_ref[b] = (t_ref[b, :, core].astype(F32) + rc_ref[b].astype(F32)).astype(BF16)

    zc = channels // nz

    def z_cols(k):
        return pl.ds(pl.multiple_of(z_peer(k) * zc, zc), zc)

    def collect(copies, own, buffer):
        total = own.astype(F32)
        for k, copy in copies:
            copy.wait_recv()
            total = total + buffer[k].astype(F32)
        return total

    for i in range(3):
        for copy in g_copies[0, i]:
            copy.wait_recv()
        turned(0, i)
    point_terms(0)
    core0 = core_out(0)
    for i in (0, 2):
        z_copies[1, i].wait_recv()
        columns_back(1, i)
    input_terms(0)
    core_in(0, core0)
    y0_copies = [
        (k, send(s_ref.at[0, dp_peer(k)], ry_ref.at[k], ss_ry.at[k], rs_ry.at[k], {"dp": dp_peer(k)}))
        for k in range(1, ndp)
    ]

    for i in (1, 0, 2):
        for copy in g_copies[1, i]:
            copy.wait_recv()
        turned(1, i)
    point_terms(1)
    core1 = core_out(1)
    core_in(1, core1)
    z1_copies = [
        (k, send(
            s_ref.at[1, :, :, z_cols(k)], rz1_ref.at[k], ss_rz.at[k], rs_rz.at[k],
            {"row": z_peer(k) * 2 + xh},
        ))
        for k in range(1, nz)
    ]
    input_terms(1)

    u0_ref[...] = collect(y0_copies, s_ref[0, y], ry_ref).astype(BF16)
    z0_copies = [
        (k, send(
            u0_ref.at[:, z_cols(k)], rz0_ref.at[k], ss_rz.at[nz + k], rs_rz.at[nz + k],
            {"row": z_peer(k) * 2 + xh},
        ))
        for k in range(1, nz)
    ]
    u1_ref[...] = collect(z1_copies, s_ref[1, :, :, z_cols(0)], rz1_ref).astype(BF16)
    y1_copies = [
        (k, send(u1_ref.at[dp_peer(k)], ry1_ref.at[k], ss_ry.at[ndp + k], rs_ry.at[ndp + k], {"dp": dp_peer(k)}))
        for k in range(1, ndp)
    ]
    v_ref[0] = collect(z0_copies, u0_ref[:, z_cols(0)], rz0_ref)
    x_copies = [[], []]
    for b in (0, 1):
        if b == 1:
            v_ref[1] = collect(y1_copies, u1_ref[y], ry1_ref)
        x_copies[b] = [
            (k, send(
                v_ref.at[b], rx_ref.at[b, k], ss_rx.at[b * 2 * nlon + k], rs_rx.at[b * 2 * nlon + k], x_peer(k)
            ))
            for k in range(1, 2 * nlon)
        ]
    width = pg_ref.shape[1]
    pick = lax.broadcasted_iota(jnp.int32, (width, zc), 1) == (
        member * width + lax.broadcasted_iota(jnp.int32, (width, zc), 0)
    )
    pick = pick.astype(F32)
    for b in (0, 1):
        sums = [v_ref[b], None]
        for k, copy in x_copies[b]:
            copy.wait_recv()
            part = rx_ref[b, k]
            sums[k % 2] = part if sums[k % 2] is None else sums[k % 2] + part
        low = jnp.where(core == 0, sums[0], sums[1])
        high = jnp.where(core == 0, sums[1], sums[0])
        block = jnp.concatenate([low, high], axis=0)
        pg_ref[b] = scale * lax.dot_general(
            pick, block, NT, preferred_element_type=F32, precision=lax.Precision.HIGHEST
        )
    for copy in started:
        copy.wait_send()


def shards(features, depthwise_kernels, point_weights, proj_weight, class_weight, labels):
    rows, cols, channels = features.shape[1:]
    outc = point_weights.shape[2]
    classes = class_weight.shape[1]
    ndp, nrow, nlon = (lax.axis_size(a) for a in ("dp", "row", "lon"))
    nz = nrow // 2
    hops = (DILATION_INNER // rows, DILATION_OUTER // rows)
    groups = cols // GROUP
    real = rows * GROUP
    gp = -(-real // 16) * 16
    pix = groups * gp
    pix_pad = -(-pix // 128) * 128
    zc = channels // nz
    half = outc // ndp // 2
    chunk = channels // (nrow * nlon)
    scale = 1.0 / math.sqrt(ndp * nrow * nlon * rows * cols)

    x = features[0].reshape(rows, groups, GROUP, channels).transpose(1, 0, 2, 3)
    x = jnp.pad(x.reshape(groups, real, channels), ((0, 0), (0, gp - real), (0, 0)))
    x = jnp.pad(x.reshape(pix, channels), ((0, pix_pad - pix), (0, 0)))
    lab = labels[0].reshape(rows, groups, GROUP).transpose(1, 0, 2).reshape(groups, real)
    lab = jnp.pad(lab, ((0, 0), (0, gp - real))).reshape(pix, 1)
    cls = jnp.pad(class_weight, ((0, 0), (0, 128 - classes)))

    vmem = pl.BlockSpec(memory_space=pltpu.VMEM)
    dma = lambda n: pltpu.SemaphoreType.DMA((n,))
    scratch = [
        pltpu.VMEM((18, channels), F32),
        pltpu.VMEM((18, 16, channels), BF16),
        pltpu.VMEM((6, pix, outc), F32),
        pltpu.VMEM((3, 2, pix, outc), BF16),
        pltpu.VMEM((3, 2, pix, outc), BF16),
        pltpu.VMEM((3, 2, gp, outc), BF16),
        pltpu.VMEM((3, 2, gp, outc), BF16),
        pltpu.VMEM((4, pix, outc), BF16),
        pltpu.VMEM((4, pix, outc), BF16),
        pltpu.VMEM((3, 5, gp, outc), BF16),
        pltpu.VMEM((3, 9, gp, outc), BF16),
        pltpu.VMEM((9, outc, pix_pad), BF16),
        pltpu.VMEM((pix, channels), F32),
        pltpu.VMEM((2, ndp, 2, half, channels), BF16),
        pltpu.VMEM((2, ndp, half, channels), BF16),
        pltpu.VMEM((2, ndp, half, channels), BF16),
        pltpu.VMEM((ndp, half, channels), BF16),
        pltpu.VMEM((half, channels), BF16),
        pltpu.VMEM((nz, half, zc), BF16),
        pltpu.VMEM((nz, ndp, half, zc), BF16),
        pltpu.VMEM((ndp, half, zc), BF16),
        pltpu.VMEM((ndp, half, zc), BF16),
        pltpu.VMEM((2, half, zc), F32),
        pltpu.VMEM((2, 2 * nlon, half, zc), F32),
        dma(12), dma(12), dma(4), dma(4), dma(4), dma(4), dma(12), dma(12),
        dma(2), dma(2), dma(2 * ndp), dma(2 * ndp), dma(2 * nz), dma(2 * nz),
        dma(4 * nlon), dma(4 * nlon),
    ]
    input_grad, point_grad = pl.pallas_call(
        functools.partial(kernel, (ndp, nrow, nlon), hops, scale),
        out_shape=(
            jax.ShapeDtypeStruct((pix, channels), BF16),
            jax.ShapeDtypeStruct((2, chunk, outc // ndp), F32),
        ),
        in_specs=[vmem] * 6,
        out_specs=(vmem, vmem),
        scratch_shapes=scratch,
        compiler_params=pltpu.CompilerParams(
            collective_id=0, has_side_effects=True, vmem_limit_bytes=56 * 1024 * 1024
        ),
        cost_estimate=pl.CostEstimate(
            flops=54 * 2 * pix * channels * outc, bytes_accessed=8 * pix * channels, transcendentals=0
        ),
    )(x, depthwise_kernels.reshape(18, channels), point_weights, proj_weight, cls, lab)
    input_grad = input_grad.reshape(groups, gp, channels)[:, :real]
    input_grad = input_grad.reshape(groups, rows, GROUP, channels).transpose(1, 0, 2, 3)
    return input_grad.reshape(1, rows, cols, channels), point_grad


def solution(mesh):
    placed = (P("dp", "row", "lon", None), P(), P(), P(), P(), P("dp", "row", "lon"))
    return jax.shard_map(
        shards,
        mesh=mesh,
        in_specs=placed,
        out_specs=(P("dp", "row", "lon", None), P(None, ("row", "lon"), "dp")),
        check_vma=False,
    )
```

```python
import functools
import math

import jax
import jax.numpy as jnp
from jax import lax
from jax.experimental import pallas as pl
from jax.experimental.pallas import tpu as pltpu
from jax.sharding import PartitionSpec as P

DILATION_INNER = 12
DILATION_OUTER = 36
GROUP = DILATION_INNER
LOSS_SCALE = 32.0
MESH = pl.DeviceIdType.MESH
NN = (((1,), (0,)), ((), ()))
NT = (((1,), (1,)), ((), ()))
F32 = jnp.float32
BF16 = jnp.bfloat16


def dot(a, b, dims=NN):
    return lax.dot_general(a, b, dims, preferred_element_type=F32)


def slope(value, sigma):
    return sigma * (1.0 + value * (1.0 - sigma))


def pixel_places(axis, shape, gp, rows, pitch):
    m = lax.broadcasted_iota(jnp.int32, shape, axis)
    zero = jnp.zeros(shape, jnp.int32)
    group = zero
    for g in (1, 2):
        group = group + jnp.where(m >= g * gp, 1, 0)
    rest = m - group * gp
    row = zero
    for r in range(1, rows):
        row = row + jnp.where(rest >= r * GROUP, 1, 0)
    col = rest - row * GROUP
    real = jnp.logical_and(rest < rows * GROUP, m < 3 * gp)
    return row, group * GROUP + col, jnp.where(real, row * pitch + group * GROUP + col, -1)


def kernel(
    size, hops, scale,
    x_hbm, k_hbm, pw_hbm, proj_hbm, cls_hbm, lab_hbm,
    ig_hbm, pg_ref,
    x_ref, k_ref, pw_ref, proj_ref, cls_ref, lab_ref, ig_ref, in_sem, out_sem,
    xs_ref, xg_ref, put_ref, ls_ref, hot_ref, clsp_ref, kf_ref, kb_ref, cacc_ref,
    yso_ref, yro_ref, ysi_ref, yri_ref,
    cs_ref, cr_ref,
    g0_ref, g1_ref, gt_ref, igacc_ref, tacc_ref,
    t_ref, rc_ref, sa_ref, sb_ref, rya_ref, rzb_ref, ua_ref, ub_ref, rza_ref, ryb_ref, v_ref, rx_ref,
    ss_y, rs_y, ss_c, rs_c, ss_gz, rs_gz, ss_gl, rs_gl,
    ss_core, rs_core, ss_ya, rs_ya, ss_zb, rs_zb, ss_za, rs_za, ss_yb, rs_yb, ss_rx, rs_rx,
):
    ndp, nrow, nlon = size
    nz = nrow // 2
    rows, cols_dev, channels = x_ref.shape
    outc = pw_ref.shape[2]
    gp = g0_ref.shape[2]
    pix = 3 * gp
    pix_pad = xg_ref.shape[0]
    pitch = xs_ref.shape[1]
    y = lax.axis_index("dp")
    row = lax.axis_index("row")
    lon = lax.axis_index("lon")
    z = row // 2
    xh = row % 2
    core = lon % 2
    member = xh * nlon + lon
    right = {"lon": (lon + 1) % nlon}
    left = {"lon": (lon + nlon - 1) % nlon}
    partner = {"lon": lon + 1 - 2 * core}

    def along(shift):
        return {"row": (row + shift + nrow) % nrow}

    def dp_peer(k):
        return (y + k) % ndp

    def z_peer(k):
        return (z + k) % nz

    def z_device(k):
        return {"row": z_peer(k) * 2 + xh}

    def x_peer(k):
        other = (member + k) % (2 * nlon)
        return {"row": z * 2 + other // nlon, "lon": other % nlon}

    started = []

    def remote(src, dst, ssem, rsem, device):
        return pltpu.make_async_remote_copy(
            src_ref=src, dst_ref=dst, send_sem=ssem, recv_sem=rsem,
            device_id=device, device_id_type=MESH,
        )

    def send(*args):
        copy = remote(*args)
        copy.start()
        started.append(copy)
        return copy

    loads = [
        pltpu.make_async_copy(src, dst, in_sem.at[n])
        for n, (src, dst) in enumerate((
            (k_hbm, k_ref), (x_hbm.at[0], x_ref), (pw_hbm, pw_ref),
            (proj_hbm, proj_ref), (cls_hbm, cls_ref), (lab_hbm, lab_ref),
        ))
    ]
    for load in loads:
        load.start()

    barrier = pltpu.get_barrier_semaphore()
    peers = [left, right]
    for shift in hops:
        peers += [along(shift), along(-shift)]
    peers += [{"dp": dp_peer(k)} for k in range(1, ndp)]
    peers += [z_device(k) for k in range(1, nz)]
    peers += [x_peer(k) for k in range(1, 2 * nlon)]
    for peer in peers:
        pl.semaphore_signal(barrier, inc=1, device_id=peer, device_id_type=MESH)

    loads[0].wait()
    for i in range(3):
        for j in range(3):
            taps_ij = k_ref[i, j].astype(F32)
            for b in (0, 1):
                t = b * 9 + i * 3 + j
                kf_ref[t : t + 1, :] = taps_ij[b : b + 1]
    for t in range(18):
        kb_ref[t] = jnp.broadcast_to(kf_ref[t : t + 1, :], (16, channels)).astype(BF16)

    loads[1].wait()
    for r in range(rows):
        xs_ref[r, pitch - 16 :, :] = jnp.zeros((16, channels), BF16)
        xs_ref[r, :cols_dev, :] = x_ref[r]
    _, _, place = pixel_places(0, (pix_pad, rows * pitch), gp, rows, pitch)
    spot = lax.broadcasted_iota(jnp.int32, place.shape, 1)
    gather = (place == spot).astype(F32).astype(BF16)
    xg_ref[...] = dot(gather, xs_ref[...].reshape(rows * pitch, channels)).astype(BF16)
    loads[2].wait()

    def tap(b, i, j):
        x = xg_ref[:pix, :].reshape(pix // 16, 16, channels)
        scaled = (x * kb_ref[b * 9 + i * 3 + j][None]).reshape(pix, channels)
        return dot(scaled, pw_ref[b])

    group_rows = [slice(g * gp, (g + 1) * gp) for g in range(3)]
    lon_copies = {}

    def outer_send(i, g):
        n = 6 + (3 * i + g) * 2
        here = group_rows[g]
        lon_copies[1, i, g] = [
            send(yso_ref.at[i, e, here], yro_ref.at[i, e, here], ss_y.at[n + e], rs_y.at[n + e], device)
            for e, device in ((0, right), (1, left))
        ]

    def outer_sides(i):
        yso_ref[i, 0] = tap(1, i, 0).astype(BF16)
        yso_ref[i, 1] = tap(1, i, 2).astype(BF16)

    def inner_taps(i):
        y0 = tap(0, i, 0)
        ysi_ref[i, 0] = y0[2 * gp :].astype(BF16)
        y2 = tap(0, i, 2)
        ysi_ref[i, 1] = y2[:gp].astype(BF16)
        lon_copies[0, i] = [
            send(ysi_ref.at[i, e], yri_ref.at[i, e], ss_y.at[2 * i + e], rs_y.at[2 * i + e], device)
            for e, device in ((0, right), (1, left))
        ]
        cacc_ref[i] = tap(0, i, 1)
        cacc_ref[i, gp:, :] += y0[: 2 * gp]
        cacc_ref[i, : 2 * gp, :] += y2[gp:]

    def outer_done(i, g):
        for copy in lon_copies[1, i, g]:
            copy.wait_recv()
        here = group_rows[g]
        return cacc_ref[3 + i, here] + yro_ref[i, 0, here].astype(F32) + yro_ref[i, 1, here].astype(F32)

    def inner_done(i, g):
        total = cacc_ref[i, group_rows[g]]
        if g == 0:
            lon_copies[0, i][0].wait_recv()
            total = total + yri_ref[i, 0].astype(F32)
        if g == 2:
            lon_copies[0, i][1].wait_recv()
            total = total + yri_ref[i, 1].astype(F32)
        return total

    row_copies = {}

    def rows_out(b, i, g):
        here = group_rows[g]
        m = 2 * b + i // 2
        cs_ref[m, here] = (inner_done, outer_done)[b](i, g).astype(BF16)
        row_copies[b, i, g] = send(
            cs_ref.at[m, here], cr_ref.at[m, here], ss_c.at[3 * m + g], rs_c.at[3 * m + g],
            along(hops[b] * (1 - i)),
        )

    outer_sides(0)
    outer_sides(2)
    pl.semaphore_wait(barrier, len(peers))
    outer_send(0, 0)
    outer_send(2, 0)
    inner_taps(0)
    inner_taps(2)
    for g in (1, 2):
        outer_send(0, g)
        outer_send(2, g)
    cacc_ref[3] = tap(1, 0, 1)
    cacc_ref[5] = tap(1, 2, 1)
    outer_sides(1)
    outer_send(1, 0)
    inner_taps(1)
    for g in (1, 2):
        outer_send(1, g)
    for g in range(3):
        for b in (1, 0):
            for i in (0, 2):
                rows_out(b, i, g)
        if g == 0:
            cacc_ref[4] = tap(1, 1, 1)

    for load in loads[3:]:
        load.wait()
    ls_ref[...] = jnp.zeros_like(ls_ref)
    for r in range(rows):
        ls_ref[r : r + 1, :cols_dev] = lab_ref[r].astype(F32)
    wide = (pix, 128)
    lane = lax.broadcasted_iota(jnp.int32, wide, 1)
    pixel_row, pixel_col, _ = pixel_places(0, wide, gp, rows, pitch)
    by_row = dot((lane == pixel_row).astype(F32).astype(BF16), ls_ref[...].astype(BF16))
    label = jnp.sum(jnp.where(lane == pixel_col, by_row, 0.0), axis=1, keepdims=True)
    hot_ref[...] = (lane.astype(F32) == label).astype(F32)
    clsp_ref[...] = jnp.zeros_like(clsp_ref)
    clsp_ref[: cls_ref.shape[0], :] = cls_ref[...]
    _, _, place = pixel_places(1, (rows * pitch, pix_pad), gp, rows, pitch)
    spot = lax.broadcasted_iota(jnp.int32, place.shape, 0)
    put_ref[...] = (place == spot).astype(F32).astype(BF16)

    def inside(source):
        return jnp.logical_and(source >= 0, source < nrow)

    def head(g):
        here = group_rows[g]
        point_pre = []
        for b in (0, 1):
            total = (inner_done, outer_done)[b](1, g)
            for i in (0, 2):
                row_copies[b, i, g].wait_recv()
                term = cr_ref[2 * b + i // 2, here].astype(F32)
                total = total + jnp.where(inside(row + hops[b] * (i - 1)), term, 0.0)
            point_pre.append(total)
        sig = [jax.nn.sigmoid(v) for v in point_pre]
        joined = jnp.concatenate([(v * s).astype(BF16) for v, s in zip(point_pre, sig)], axis=1)
        proj_pre = dot(joined, proj_ref[...])
        proj_sig = jax.nn.sigmoid(proj_pre)
        projected = (proj_pre * proj_sig).astype(BF16)
        logits = dot(projected, clsp_ref[...], NT)
        real = lax.broadcasted_iota(jnp.int32, logits.shape, 1) < cls_ref.shape[0]
        top = jnp.max(jnp.where(real, logits, -jnp.inf), axis=1, keepdims=True)
        power = jnp.where(real, jnp.exp(jnp.where(real, logits - top, 0.0)), 0.0)
        soft = power / jnp.sum(power, axis=1, keepdims=True)
        grad_logits = (LOSS_SCALE * (soft - hot_ref[here])).astype(BF16)
        grad_proj = (dot(grad_logits, clsp_ref[...]) * slope(proj_pre, proj_sig)).astype(BF16)
        grad_joined = dot(grad_proj, proj_ref[...], NT)
        return [
            (grad_joined[:, b * outc : (b + 1) * outc] * slope(point_pre[b], sig[b])).astype(BF16)
            for b in (0, 1)
        ]

    z_copies = {}
    g_copies = {}

    def rows_back(b, i, g):
        ref = (g0_ref, g1_ref)[b]
        own = slice(1 + 2 * b + g, 2 + 2 * b + g)
        n = 3 * (2 * b + i // 2) + g
        z_copies[b, i, g] = send(
            ref.at[1, own], ref.at[i, own], ss_gz.at[n], rs_gz.at[n], along(hops[b] * (i - 1))
        )

    def inner_side(i, g):
        if g == 1:
            return
        src, dst, e, device = (
            (slice(3, 4), slice(0, 1), 0, right) if g == 2 else (slice(1, 2), slice(4, 5), 1, left)
        )
        g_copies[0, i, g] = [
            send(g0_ref.at[i, src], g0_ref.at[i, dst], ss_gl.at[2 * i + e], rs_gl.at[2 * i + e], device)
        ]

    def outer_side(i, g):
        n = 6 + 2 * (3 * i + g)
        src = slice(3 + g, 4 + g)
        g_copies[1, i, g] = [
            send(g1_ref.at[i, src], g1_ref.at[i, dst], ss_gl.at[n + e], rs_gl.at[n + e], device)
            for e, (dst, device) in enumerate(((slice(g, g + 1), right), (slice(6 + g, 7 + g), left)))
        ]

    for g in range(3):
        grads = head(g)
        g0_ref[1, 1 + g] = grads[0]
        g1_ref[1, 3 + g] = grads[1]
        for b in (0, 1):
            for i in (0, 2):
                rows_back(b, i, g)
        inner_side(1, g)
        outer_side(1, g)

    def pass_on(b, g):
        for i in (0, 2):
            z_copies[b, i, g].wait_recv()
            (inner_side, outer_side)[b](i, g)

    for b in (0, 1):
        for i in (0, 2):
            first = b * 9 + i * 3
            keep = inside(row - hops[b] * (i - 1)).astype(F32)
            kf_ref[first : first + 3, :] = kf_ref[first : first + 3, :] * keep

    zc = channels // nz
    hc = zc // 2
    half_rows = outc // ndp // 2

    def turned(b, i, j, slot):
        start = 2 - j if b == 0 else 3 * (2 - j)
        block = (g0_ref, g1_ref)[b][i, start : start + 3].reshape(pix, outc).astype(F32)
        block = jnp.concatenate([block, jnp.zeros((pix_pad - pix, outc), F32)], axis=0)
        gt_ref[slot] = block.T.astype(BF16)

    def z_cols(k):
        return pl.ds(pl.multiple_of(z_peer(k) * zc, zc), zc)

    def core_copy(b, k):
        n = z_peer(k)
        return remote(
            t_ref.at[b, n, 1 - core], rc_ref.at[b, n],
            ss_core.at[b * nz + k], rs_core.at[b * nz + k], partner,
        )

    def zb_copy(b, k):
        return remote(
            sb_ref.at[b, z_peer(k)], rzb_ref.at[b, k],
            ss_zb.at[b * nz + k], rs_zb.at[b * nz + k], z_device(k),
        )

    def point_terms(b, taps, first, last, steps=(0, None)):
        def step(s, carry):
            k = (s + 1) % nz
            cols = z_cols(k)
            terms = dot(gt_ref[: len(taps)].reshape(len(taps) * outc, pix_pad), xg_ref[:, cols])
            total = None if first else tacc_ref[:, cols]
            for slot, (i, j) in enumerate(taps):
                t = b * 9 + i * 3 + j
                term = terms[slot * outc : (slot + 1) * outc] * kf_ref[t : t + 1, cols]
                total = term if total is None else total + term
            if not last:
                tacc_ref[:, cols] = total
            else:
                block = total.astype(BF16).reshape(ndp, 2, half_rows, zc)
                for c in (0, 1):
                    t_ref[b, z_peer(k), c] = block[:, c]
                core_copy(b, k).start()
            return carry

        lax.fori_loop(steps[0], nz if steps[1] is None else steps[1], step, 0)

    def chip_sums(b):
        def add(k):
            core_copy(b, k).wait_recv()
            n = z_peer(k)
            total = (t_ref[b, n, core].astype(F32) + rc_ref[b, n].astype(F32)).astype(BF16)
            sb_ref[b, n] = total[:, :, hc:]
            sa_ref[b, :, n] = total[:, :, :hc]

        def step(s, carry):
            add(s + 1)
            zb_copy(b, s + 1).start()
            return carry

        lax.fori_loop(0, nz - 1, step, 0)
        add(0)
        return [
            (k, send(
                sa_ref.at[b, dp_peer(k)], rya_ref.at[b, k],
                ss_ya.at[b * ndp + k], rs_ya.at[b * ndp + k], {"dp": dp_peer(k)},
            ))
            for k in range(1, ndp)
        ]

    def collect(copies, own, buffer):
        total = own.astype(F32)
        for k, copy in copies:
            copy.wait_recv()
            total = total + buffer[k].astype(F32)
        return total

    def second(b, ya):
        ua_ref[b] = collect(ya, sa_ref[b, y], rya_ref.at[b]).astype(BF16)
        za = [
            (k, send(
                ua_ref.at[b, z_peer(k)], rza_ref.at[b, k],
                ss_za.at[b * nz + k], rs_za.at[b * nz + k], z_device(k),
            ))
            for k in range(1, nz)
        ]
        zb = [(k, zb_copy(b, k)) for k in range(1, nz)]
        ub_ref[b] = collect(zb, sb_ref[b, z], rzb_ref.at[b]).astype(BF16)
        yb = [
            (k, send(
                ub_ref.at[b, dp_peer(k)], ryb_ref.at[b, k],
                ss_yb.at[b * ndp + k], rs_yb.at[b * ndp + k], {"dp": dp_peer(k)},
            ))
            for k in range(1, ndp)
        ]
        return za, yb

    def third(b, za, yb):
        part_a = collect(za, ua_ref[b, z], rza_ref.at[b])
        part_b = collect(yb, ub_ref[b, y], ryb_ref.at[b])
        v_ref[b] = jnp.concatenate([part_a, part_b], axis=1).astype(BF16)
        return [
            (k, send(
                v_ref.at[b], rx_ref.at[b, k],
                ss_rx.at[b * 2 * nlon + k], rs_rx.at[b * 2 * nlon + k], x_peer(k),
            ))
            for k in range(1, 2 * nlon)
        ]

    def input_terms(b):
        def step(n, carry):
            cols = pl.ds(pl.multiple_of(n * zc, zc), zc)
            weights = pw_ref[b, cols, :]
            total = None
            for i in range(3):
                if b == 0:
                    spread = dot(g0_ref[i].reshape(5 * gp, outc), weights, NT)
                else:
                    spread = dot(g1_ref[i].reshape(9 * gp, outc), weights, NT)
                for j in range(3):
                    start = (2 - j) * gp if b == 0 else (2 - j) * pix
                    t = b * 9 + 3 * i + j
                    term = spread[start : start + pix] * kf_ref[t : t + 1, cols]
                    total = term if total is None else total + term
            if b == 0:
                igacc_ref[:, cols] = total
            else:
                total = (igacc_ref[:, cols] + total).astype(BF16)
                total = jnp.concatenate([total, jnp.zeros((pix_pad - pix, zc), BF16)], axis=0)
                placed = dot(put_ref[...], total).astype(BF16)
                for r in range(rows):
                    ig_ref[r, :, cols] = placed[r * pitch : r * pitch + cols_dev]
            return carry

        lax.fori_loop(0, nz, step, 0)

    pass_on(0, 0)
    pass_on(1, 0)
    for g in range(3):
        for copy in g_copies[1, 1, g]:
            copy.wait_recv()
    for j in range(3):
        turned(1, 1, j, j)
    point_terms(1, [(1, j) for j in range(3)], True, False)
    pass_on(0, 1)
    pass_on(1, 1)
    pass_on(0, 2)
    for i in range(3):
        for g in (0, 2):
            for copy in g_copies[0, i, g]:
                copy.wait_recv()
        for j in range(3):
            turned(0, i, j, 3 * i + j)
    inner = [(i, j) for i in range(3) for j in range(3)]
    point_terms(0, inner, True, True, (0, nz // 2))
    pass_on(1, 2)
    point_terms(0, inner, True, True, (nz // 2, nz))
    ya0 = chip_sums(0)
    middle = [(0, 1), (2, 1)]
    for slot, (i, j) in enumerate(middle):
        turned(1, i, j, slot)
    point_terms(1, middle, False, False)
    sides = [(i, j) for i in (0, 2) for j in (0, 2)]
    for i in (0, 2):
        for g in range(3):
            for copy in g_copies[1, i, g]:
                copy.wait_recv()
    for slot, (i, j) in enumerate(sides):
        turned(1, i, j, slot)
    point_terms(1, sides, False, True)
    ya1 = chip_sums(1)
    input_terms(0)
    za0, yb0 = second(0, ya0)
    input_terms(1)
    ig_out = pltpu.make_async_copy(ig_ref, ig_hbm.at[0], out_sem)
    ig_out.start()

    za1, yb1 = second(1, ya1)
    x_copies = [third(0, za0, yb0)]
    x_copies.append(third(1, za1, yb1))
    width = pg_ref.shape[1]
    pick = lax.broadcasted_iota(jnp.int32, (width, zc), 1) == (
        member * width + lax.broadcasted_iota(jnp.int32, (width, zc), 0)
    )
    pick = pick.astype(F32)
    for b in (0, 1):
        sums = [v_ref[b].astype(F32), None]
        for k, copy in x_copies[b]:
            copy.wait_recv()
            part = rx_ref[b, k].astype(F32)
            sums[k % 2] = part if sums[k % 2] is None else sums[k % 2] + part
        low = jnp.where(core == 0, sums[0], sums[1])
        high = jnp.where(core == 0, sums[1], sums[0])
        block = jnp.concatenate([low, high], axis=0)
        pg_ref[b] = scale * lax.dot_general(
            pick, block, NT, preferred_element_type=F32, precision=lax.Precision.HIGHEST
        )
    ig_out.wait()
    for copy in started:
        copy.wait_send()

    def finish(k, carry):
        for b in (0, 1):
            core_copy(b, k).wait_send()
        return carry

    lax.fori_loop(0, nz, finish, 0)

    def finish_z(k, carry):
        for b in (0, 1):
            zb_copy(b, k).wait_send()
        return carry

    lax.fori_loop(1, nz, finish_z, 0)


def shards(features, depthwise_kernels, point_weights, proj_weight, class_weight, labels):
    rows, cols, channels = features.shape[1:]
    outc = point_weights.shape[2]
    ndp, nrow, nlon = (lax.axis_size(a) for a in ("dp", "row", "lon"))
    nz = nrow // 2
    hops = (DILATION_INNER // rows, DILATION_OUTER // rows)
    groups = cols // GROUP
    gp = -(-rows * GROUP // 16) * 16
    pix = groups * gp
    pix_pad = -(-pix // 128) * 128
    pitch = -(-cols // 16) * 16
    zc = channels // nz
    hc = zc // 2
    half = outc // ndp // 2
    chunk = channels // (nrow * nlon)
    scale = 1.0 / math.sqrt(ndp * nrow * nlon * rows * cols)

    vmem = pl.BlockSpec(memory_space=pltpu.VMEM)
    hbm = pl.BlockSpec(memory_space=pl.ANY)
    kernels = depthwise_kernels.transpose(1, 2, 0, 3)
    classes = class_weight.T
    label_rows = labels.transpose(1, 0, 2)
    dma = lambda n: pltpu.SemaphoreType.DMA((n,))
    scratch = [
        pltpu.VMEM(features.shape[1:], BF16),
        pltpu.VMEM(kernels.shape, BF16),
        pltpu.VMEM(point_weights.shape, BF16),
        pltpu.VMEM(proj_weight.shape, BF16),
        pltpu.VMEM(classes.shape, BF16),
        pltpu.VMEM(label_rows.shape, jnp.int32),
        pltpu.VMEM(features.shape[1:], BF16),
        dma(6), pltpu.SemaphoreType.DMA,
        pltpu.VMEM((rows, pitch, channels), BF16),
        pltpu.VMEM((pix_pad, channels), BF16),
        pltpu.VMEM((rows * pitch, pix_pad), BF16),
        pltpu.VMEM((128, 128), F32),
        pltpu.VMEM((pix, 128), F32),
        pltpu.VMEM((128, outc), BF16),
        pltpu.VMEM((18, channels), F32),
        pltpu.VMEM((18, 16, channels), BF16),
        pltpu.VMEM((6, pix, outc), F32),
        pltpu.VMEM((3, 2, pix, outc), BF16),
        pltpu.VMEM((3, 2, pix, outc), BF16),
        pltpu.VMEM((3, 2, gp, outc), BF16),
        pltpu.VMEM((3, 2, gp, outc), BF16),
        pltpu.VMEM((4, pix, outc), BF16),
        pltpu.VMEM((4, pix, outc), BF16),
        pltpu.VMEM((3, 5, gp, outc), BF16),
        pltpu.VMEM((3, 9, gp, outc), BF16),
        pltpu.VMEM((9, outc, pix_pad), BF16),
        pltpu.VMEM((pix, channels), F32),
        pltpu.VMEM((outc, channels), F32),
        pltpu.VMEM((2, nz, 2, ndp, half, zc), BF16),
        pltpu.VMEM((2, nz, ndp, half, zc), BF16),
        pltpu.VMEM((2, ndp, nz, half, hc), BF16),
        pltpu.VMEM((2, nz, ndp, half, hc), BF16),
        pltpu.VMEM((2, ndp, nz, half, hc), BF16),
        pltpu.VMEM((2, nz, ndp, half, hc), BF16),
        pltpu.VMEM((2, nz, half, hc), BF16),
        pltpu.VMEM((2, ndp, half, hc), BF16),
        pltpu.VMEM((2, nz, half, hc), BF16),
        pltpu.VMEM((2, ndp, half, hc), BF16),
        pltpu.VMEM((2, half, zc), BF16),
        pltpu.VMEM((2, 2 * nlon, half, zc), BF16),
        dma(24), dma(24), dma(12), dma(12), dma(12), dma(12), dma(24), dma(24),
        dma(2 * nz), dma(2 * nz), dma(2 * ndp), dma(2 * ndp), dma(2 * nz), dma(2 * nz),
        dma(2 * nz), dma(2 * nz), dma(2 * ndp), dma(2 * ndp), dma(4 * nlon), dma(4 * nlon),
    ]
    return pl.pallas_call(
        functools.partial(kernel, (ndp, nrow, nlon), hops, scale),
        out_shape=(
            jax.ShapeDtypeStruct(features.shape, BF16),
            jax.ShapeDtypeStruct((2, chunk, outc // ndp), F32),
        ),
        in_specs=[hbm] * 6,
        out_specs=(hbm, vmem),
        scratch_shapes=scratch,
        compiler_params=pltpu.CompilerParams(
            collective_id=0, has_side_effects=True, vmem_limit_bytes=56 * 1024 * 1024
        ),
        cost_estimate=pl.CostEstimate(
            flops=54 * 2 * pix * channels * outc, bytes_accessed=8 * pix * channels, transcendentals=0
        ),
    )(features, kernels, point_weights, proj_weight, classes, label_rows)


def solution(mesh):
    placed = (P("dp", "row", "lon", None), P(), P(), P(), P(), P("dp", "row", "lon"))
    return jax.shard_map(
        shards,
        mesh=mesh,
        in_specs=placed,
        out_specs=(P("dp", "row", "lon", None), P(None, ("row", "lon"), "dp")),
        check_vma=False,
    )
```

```python
import functools
import math

import jax
import jax.numpy as jnp
from jax import lax
from jax.experimental import pallas as pl
from jax.experimental.pallas import tpu as pltpu
from jax.sharding import PartitionSpec as P

DILATION_INNER = 12
DILATION_OUTER = 36
GROUP = DILATION_INNER
LOSS_SCALE = 32.0
MESH = pl.DeviceIdType.MESH
NN = (((1,), (0,)), ((), ()))
NT = (((1,), (1,)), ((), ()))
F32 = jnp.float32
BF16 = jnp.bfloat16


def dot(a, b, dims=NN):
    return lax.dot_general(a, b, dims, preferred_element_type=F32)


def slope(value, sigma):
    return sigma * (1.0 + value * (1.0 - sigma))


def pixel_places(axis, shape, gp, rows, pitch):
    m = lax.broadcasted_iota(jnp.int32, shape, axis)
    zero = jnp.zeros(shape, jnp.int32)
    group = zero
    for g in (1, 2):
        group = group + jnp.where(m >= g * gp, 1, 0)
    rest = m - group * gp
    row = zero
    for r in range(1, rows):
        row = row + jnp.where(rest >= r * GROUP, 1, 0)
    col = rest - row * GROUP
    real = jnp.logical_and(rest < rows * GROUP, m < 3 * gp)
    return row, group * GROUP + col, jnp.where(real, row * pitch + group * GROUP + col, -1)


def kernel(
    size, hops, scale,
    x_hbm, k_hbm, pw_hbm, proj_hbm, cls_hbm, lab_hbm,
    ig_hbm, pg_ref,
    x_ref, k_ref, pw_ref, proj_ref, cls_ref, lab_ref, ig_ref, in_sem, out_sem,
    xs_ref, xg_ref, put_ref, ls_ref, hot_ref, clsp_ref, kf_ref, kb_ref, cacc_ref,
    yso_ref, yro_ref, ysi_ref, yri_ref,
    cs_ref, cr_ref,
    g0_ref, g1_ref, gt_ref, igacc_ref, tacc_ref,
    t_ref, rc_ref, sa_ref, sb_ref, rya_ref, rzb_ref, ua_ref, ub_ref, rza_ref, ryb_ref, v_ref, rx_ref,
    ss_y, rs_y, ss_c, rs_c, ss_gz, rs_gz, ss_gl, rs_gl,
    ss_core, rs_core, ss_ya, rs_ya, ss_zb, rs_zb, ss_za, rs_za, ss_yb, rs_yb, ss_rx, rs_rx,
):
    ndp, nrow, nlon = size
    nz = nrow // 2
    rows, cols_dev, channels = x_ref.shape
    outc = pw_ref.shape[2]
    gp = g0_ref.shape[2]
    pix = 3 * gp
    pix_pad = xg_ref.shape[0]
    pitch = xs_ref.shape[1]
    y = lax.axis_index("dp")
    row = lax.axis_index("row")
    lon = lax.axis_index("lon")
    z = row // 2
    xh = row % 2
    core = lon % 2
    member = xh * nlon + lon
    right = {"lon": (lon + 1) % nlon}
    left = {"lon": (lon + nlon - 1) % nlon}
    partner = {"lon": lon + 1 - 2 * core}

    def along(shift):
        return {"row": (row + shift + nrow) % nrow}

    def dp_peer(k):
        return (y + k) % ndp

    def z_peer(k):
        return (z + k) % nz

    def z_device(k):
        return {"row": z_peer(k) * 2 + xh}

    def x_peer(k):
        other = (member + k) % (2 * nlon)
        return {"row": z * 2 + other // nlon, "lon": other % nlon}

    def far_first(step, count):
        return count // 2 + (step + 1) // 2 * (1 - 2 * (step % 2))

    started = []

    def remote(src, dst, ssem, rsem, device):
        return pltpu.make_async_remote_copy(
            src_ref=src, dst_ref=dst, send_sem=ssem, recv_sem=rsem,
            device_id=device, device_id_type=MESH,
        )

    def send(*args):
        copy = remote(*args)
        copy.start()
        started.append(copy)
        return copy

    loads = [
        pltpu.make_async_copy(src, dst, in_sem.at[n])
        for n, (src, dst) in enumerate((
            (k_hbm, k_ref), (x_hbm.at[0], x_ref), (pw_hbm.at[1], pw_ref.at[1]), (pw_hbm.at[0], pw_ref.at[0]),
            (proj_hbm, proj_ref), (cls_hbm, cls_ref), (lab_hbm, lab_ref),
        ))
    ]
    for load in loads:
        load.start()

    barrier = pltpu.get_barrier_semaphore()
    peers = [left, right]
    for shift in hops:
        peers += [along(shift), along(-shift)]
    peers += [{"dp": dp_peer(k)} for k in range(1, ndp)]
    peers += [z_device(k) for k in range(1, nz)]
    peers += [x_peer(k) for k in range(1, 2 * nlon)]
    for peer in peers:
        pl.semaphore_signal(barrier, inc=1, device_id=peer, device_id_type=MESH)

    loads[0].wait()
    for i in range(3):
        for j in range(3):
            taps_ij = k_ref[i, j].astype(F32)
            for b in (0, 1):
                t = b * 9 + i * 3 + j
                kf_ref[t : t + 1, :] = taps_ij[b : b + 1]
    for t in range(18):
        kb_ref[t] = jnp.broadcast_to(kf_ref[t : t + 1, :], (16, channels)).astype(BF16)

    loads[1].wait()
    for r in range(rows):
        xs_ref[r, pitch - 16 :, :] = jnp.zeros((16, channels), BF16)
        xs_ref[r, :cols_dev, :] = x_ref[r]
    _, _, place = pixel_places(0, (pix_pad, rows * pitch), gp, rows, pitch)
    spot = lax.broadcasted_iota(jnp.int32, place.shape, 1)
    gather = (place == spot).astype(F32).astype(BF16)
    xg_ref[...] = dot(gather, xs_ref[...].reshape(rows * pitch, channels)).astype(BF16)
    loads[2].wait()

    def tap(b, i, j):
        x = xg_ref[:pix, :].reshape(pix // 16, 16, channels)
        scaled = (x * kb_ref[b * 9 + i * 3 + j][None]).reshape(pix, channels)
        return dot(scaled, pw_ref[b])

    group_rows = [slice(g * gp, (g + 1) * gp) for g in range(3)]
    lon_copies = {}

    def outer_send(i, g):
        n = 6 + (3 * i + g) * 2
        here = group_rows[g]
        lon_copies[1, i, g] = [
            send(yso_ref.at[i, e, here], yro_ref.at[i, e, here], ss_y.at[n + e], rs_y.at[n + e], device)
            for e, device in ((0, right), (1, left))
        ]

    def outer_sides(i):
        yso_ref[i, 0] = tap(1, i, 0).astype(BF16)
        yso_ref[i, 1] = tap(1, i, 2).astype(BF16)

    def inner_taps(i):
        y0 = tap(0, i, 0)
        ysi_ref[i, 0] = y0[2 * gp :].astype(BF16)
        y2 = tap(0, i, 2)
        ysi_ref[i, 1] = y2[:gp].astype(BF16)
        lon_copies[0, i] = [
            send(ysi_ref.at[i, e], yri_ref.at[i, e], ss_y.at[2 * i + e], rs_y.at[2 * i + e], device)
            for e, device in ((0, right), (1, left))
        ]
        cacc_ref[i] = tap(0, i, 1)
        cacc_ref[i, gp:, :] += y0[: 2 * gp]
        cacc_ref[i, : 2 * gp, :] += y2[gp:]

    def outer_done(i, g):
        for copy in lon_copies[1, i, g]:
            copy.wait_recv()
        here = group_rows[g]
        return cacc_ref[3 + i, here] + yro_ref[i, 0, here].astype(F32) + yro_ref[i, 1, here].astype(F32)

    def inner_done(i, g):
        total = cacc_ref[i, group_rows[g]]
        if g == 0:
            lon_copies[0, i][0].wait_recv()
            total = total + yri_ref[i, 0].astype(F32)
        if g == 2:
            lon_copies[0, i][1].wait_recv()
            total = total + yri_ref[i, 1].astype(F32)
        return total

    row_copies = {}

    def rows_out(b, i, g):
        here = group_rows[g]
        m = 2 * b + i // 2
        cs_ref[m, here] = (inner_done, outer_done)[b](i, g).astype(BF16)
        row_copies[b, i, g] = send(
            cs_ref.at[m, here], cr_ref.at[m, here], ss_c.at[3 * m + g], rs_c.at[3 * m + g],
            along(hops[b] * (1 - i)),
        )

    outer_sides(0)
    pl.semaphore_wait(barrier, len(peers))
    outer_send(0, 0)
    outer_sides(2)
    outer_send(2, 0)
    loads[3].wait()
    inner_taps(0)
    inner_taps(2)
    for g in (1, 2):
        outer_send(0, g)
        outer_send(2, g)
    cacc_ref[3] = tap(1, 0, 1)
    cacc_ref[5] = tap(1, 2, 1)
    outer_sides(1)
    outer_send(1, 0)
    inner_taps(1)
    for g in (1, 2):
        outer_send(1, g)
    for g in range(3):
        for b in (1, 0):
            for i in (0, 2):
                rows_out(b, i, g)
        if g == 0:
            cacc_ref[4] = tap(1, 1, 1)

    for load in loads[4:]:
        load.wait()
    ls_ref[...] = jnp.zeros_like(ls_ref)
    for r in range(rows):
        ls_ref[r : r + 1, :cols_dev] = lab_ref[r].astype(F32)
    wide = (pix, 128)
    lane = lax.broadcasted_iota(jnp.int32, wide, 1)
    pixel_row, pixel_col, _ = pixel_places(0, wide, gp, rows, pitch)
    by_row = dot((lane == pixel_row).astype(F32).astype(BF16), ls_ref[...].astype(BF16))
    label = jnp.sum(jnp.where(lane == pixel_col, by_row, 0.0), axis=1, keepdims=True)
    hot_ref[...] = (lane.astype(F32) == label).astype(F32)
    clsp_ref[...] = jnp.zeros_like(clsp_ref)
    clsp_ref[: cls_ref.shape[0], :] = cls_ref[...]
    _, _, place = pixel_places(1, (rows * pitch, pix_pad), gp, rows, pitch)
    spot = lax.broadcasted_iota(jnp.int32, place.shape, 0)
    put_ref[...] = (place == spot).astype(F32).astype(BF16)

    def inside(source):
        return jnp.logical_and(source >= 0, source < nrow)

    def head(g):
        here = group_rows[g]
        point_pre = []
        for b in (0, 1):
            total = (inner_done, outer_done)[b](1, g)
            for i in (0, 2):
                row_copies[b, i, g].wait_recv()
                term = cr_ref[2 * b + i // 2, here].astype(F32)
                total = total + jnp.where(inside(row + hops[b] * (i - 1)), term, 0.0)
            point_pre.append(total)
        sig = [jax.nn.sigmoid(v) for v in point_pre]
        joined = jnp.concatenate([(v * s).astype(BF16) for v, s in zip(point_pre, sig)], axis=1)
        proj_pre = dot(joined, proj_ref[...])
        proj_sig = jax.nn.sigmoid(proj_pre)
        projected = (proj_pre * proj_sig).astype(BF16)
        logits = dot(projected, clsp_ref[...], NT)
        real = lax.broadcasted_iota(jnp.int32, logits.shape, 1) < cls_ref.shape[0]
        top = jnp.max(jnp.where(real, logits, -jnp.inf), axis=1, keepdims=True)
        power = jnp.where(real, jnp.exp(jnp.where(real, logits - top, 0.0)), 0.0)
        soft = power / jnp.sum(power, axis=1, keepdims=True)
        grad_logits = (LOSS_SCALE * (soft - hot_ref[here])).astype(BF16)
        grad_proj = (dot(grad_logits, clsp_ref[...]) * slope(proj_pre, proj_sig)).astype(BF16)
        grad_joined = dot(grad_proj, proj_ref[...], NT)
        return [
            (grad_joined[:, b * outc : (b + 1) * outc] * slope(point_pre[b], sig[b])).astype(BF16)
            for b in (0, 1)
        ]

    z_copies = {}
    g_copies = {}

    def rows_back(b, i, g):
        ref = (g0_ref, g1_ref)[b]
        own = slice(1 + 2 * b + g, 2 + 2 * b + g)
        n = 3 * (2 * b + i // 2) + g
        z_copies[b, i, g] = send(
            ref.at[1, own], ref.at[i, own], ss_gz.at[n], rs_gz.at[n], along(hops[b] * (i - 1))
        )

    def inner_side(i, g):
        if g == 1:
            return
        src, dst, e, device = (
            (slice(3, 4), slice(0, 1), 0, right) if g == 2 else (slice(1, 2), slice(4, 5), 1, left)
        )
        g_copies[0, i, g] = [
            send(g0_ref.at[i, src], g0_ref.at[i, dst], ss_gl.at[2 * i + e], rs_gl.at[2 * i + e], device)
        ]

    def outer_side(i, g):
        n = 6 + 2 * (3 * i + g)
        src = slice(3 + g, 4 + g)
        g_copies[1, i, g] = [
            send(g1_ref.at[i, src], g1_ref.at[i, dst], ss_gl.at[n + e], rs_gl.at[n + e], device)
            for e, (dst, device) in enumerate(((slice(g, g + 1), right), (slice(6 + g, 7 + g), left)))
        ]

    order = (((0, 0), (1, 0)), ((0, 1),), ((0, 2), (1, 1), (1, 2)))
    for g in range(3):
        grads = head(g)
        g0_ref[1, 1 + g] = grads[0]
        g1_ref[1, 3 + g] = grads[1]
        for b, at in order[g]:
            for i in (0, 2):
                rows_back(b, i, at)
        inner_side(1, g)
        outer_side(1, g)

    def pass_on(b, g):
        for i in (0, 2):
            z_copies[b, i, g].wait_recv()
            (inner_side, outer_side)[b](i, g)

    for b in (0, 1):
        for i in (0, 2):
            first = b * 9 + i * 3
            keep = inside(row - hops[b] * (i - 1)).astype(F32)
            kf_ref[first : first + 3, :] = kf_ref[first : first + 3, :] * keep

    dp_order = [far_first(s, ndp) for s in range(ndp - 1)]
    z_order = [far_first(s, nz) for s in range(nz - 1)]
    zc = channels // nz
    hc = zc // 2
    half_rows = outc // ndp // 2

    def turned(b, i, j, slot):
        start = 2 - j if b == 0 else 3 * (2 - j)
        block = (g0_ref, g1_ref)[b][i, start : start + 3].reshape(pix, outc).astype(F32)
        block = jnp.concatenate([block, jnp.zeros((pix_pad - pix, outc), F32)], axis=0)
        gt_ref[slot] = block.T.astype(BF16)

    def z_cols(k):
        return pl.ds(pl.multiple_of(z_peer(k) * zc, zc), zc)

    def core_copy(b, k):
        n = z_peer(k)
        return remote(
            t_ref.at[b, n, 1 - core], rc_ref.at[b, n],
            ss_core.at[b * nz + k], rs_core.at[b * nz + k], partner,
        )

    def zb_copy(b, k):
        return remote(
            sb_ref.at[b, z_peer(k)], rzb_ref.at[b, k],
            ss_zb.at[b * nz + k], rs_zb.at[b * nz + k], z_device(k),
        )

    def point_tile(b, taps, first, cols):
        terms = dot(gt_ref[: len(taps)].reshape(len(taps) * outc, pix_pad), xg_ref[:, cols])
        total = None if first else tacc_ref[b, :, cols]
        for slot, (i, j) in enumerate(taps):
            t = b * 9 + i * 3 + j
            term = terms[slot * outc : (slot + 1) * outc] * kf_ref[t : t + 1, cols]
            total = term if total is None else total + term
        return total

    def point_terms(b, taps, first):
        for slot, (i, j) in enumerate(taps):
            turned(b, i, j, slot)

        def step(n, carry):
            cols = pl.ds(pl.multiple_of(n * zc, zc), zc)
            tacc_ref[b, :, cols] = point_tile(b, taps, first, cols)
            return carry

        lax.fori_loop(0, nz, step, 0)

    def point_last(b, taps):
        for slot, (i, j) in enumerate(taps):
            turned(b, i, j, slot)

        def step(s, carry):
            k = far_first(s, nz)
            block = point_tile(b, taps, False, z_cols(k)).astype(BF16).reshape(ndp, 2, half_rows, zc)
            for c in (0, 1):
                t_ref[b, z_peer(k), c] = block[:, c]
            core_copy(b, k).start()
            return carry

        lax.fori_loop(0, nz, step, 0)

    def chip_sums(b):
        def add(k, slot):
            core_copy(b, k).wait_recv()
            n = z_peer(k)
            total = (t_ref[b, n, core].astype(F32) + rc_ref[b, n].astype(F32)).astype(BF16)
            sb_ref[b, n] = total[:, :, hc:]
            sa_ref[b, :, slot] = total[:, :, :hc]

        def step(s, carry):
            k = far_first(s, nz)
            add(k, s)
            zb_copy(b, k).start()
            return carry

        def to_dp(part):
            here = slice(0, nz // 2) if part == 0 else slice(nz // 2, nz)
            return [
                (k, send(
                    sa_ref.at[b, dp_peer(k), here], rya_ref.at[b, k, here],
                    ss_ya.at[(2 * b + part) * ndp + k], rs_ya.at[(2 * b + part) * ndp + k],
                    {"dp": dp_peer(k)},
                ))
                for k in dp_order
            ]

        lax.fori_loop(0, nz // 2, step, 0)
        ya = to_dp(0)
        lax.fori_loop(nz // 2, nz - 1, step, 0)
        add(0, nz - 1)
        return ya + to_dp(1)

    def collect(copies, own, buffer):
        total = own.astype(F32)
        for k, copy in copies:
            copy.wait_recv()
            total = total + buffer[k].astype(F32)
        return total

    def second(b, ya):
        for _, copy in ya:
            copy.wait_recv()
        total = sa_ref[b, y].astype(F32)
        for k in range(1, ndp):
            total = total + rya_ref[b, k].astype(F32)
        ua_ref[b] = total.astype(BF16)
        za = [
            (k, send(
                ua_ref.at[b, s], rza_ref.at[b, k],
                ss_za.at[b * nz + k], rs_za.at[b * nz + k], z_device(k),
            ))
            for s, k in enumerate(z_order)
        ]
        zb = [(k, zb_copy(b, k)) for k in range(1, nz)]
        ub_ref[b] = collect(zb, sb_ref[b, z], rzb_ref.at[b]).astype(BF16)
        yb = [
            (k, send(
                ub_ref.at[b, dp_peer(k)], ryb_ref.at[b, k],
                ss_yb.at[b * ndp + k], rs_yb.at[b * ndp + k], {"dp": dp_peer(k)},
            ))
            for k in dp_order
        ]
        return za, yb

    def third(b, za, yb):
        part_a = collect(za, ua_ref[b, nz - 1], rza_ref.at[b])
        part_b = collect(yb, ub_ref[b, y], ryb_ref.at[b])
        v_ref[b] = jnp.concatenate([part_a, part_b], axis=1).astype(BF16)
        return [
            (k, send(
                v_ref.at[b], rx_ref.at[b, k],
                ss_rx.at[b * 2 * nlon + k], rs_rx.at[b * 2 * nlon + k], x_peer(k),
            ))
            for k in range(1, 2 * nlon)
        ]

    def input_terms(b):
        def step(n, carry):
            cols = pl.ds(pl.multiple_of(n * zc, zc), zc)
            weights = pw_ref[b, cols, :]
            total = None
            for i in range(3):
                if b == 0:
                    spread = dot(g0_ref[i].reshape(5 * gp, outc), weights, NT)
                else:
                    spread = dot(g1_ref[i].reshape(9 * gp, outc), weights, NT)
                for j in range(3):
                    start = (2 - j) * gp if b == 0 else (2 - j) * pix
                    t = b * 9 + 3 * i + j
                    term = spread[start : start + pix] * kf_ref[t : t + 1, cols]
                    total = term if total is None else total + term
            if b == 0:
                igacc_ref[:, cols] = total
            else:
                total = (igacc_ref[:, cols] + total).astype(BF16)
                total = jnp.concatenate([total, jnp.zeros((pix_pad - pix, zc), BF16)], axis=0)
                placed = dot(put_ref[...], total).astype(BF16)
                for r in range(rows):
                    ig_ref[r, :, cols] = placed[r * pitch : r * pitch + cols_dev]
            return carry

        lax.fori_loop(0, nz, step, 0)

    across = [(1, j) for j in range(3)]
    middle = [(0, 1), (2, 1)]
    sides = [(i, j) for i in (0, 2) for j in (0, 2)]

    def arrived(b, i):
        for g in (range(3) if b == 1 else (0, 2)):
            for copy in g_copies[b, i, g]:
                copy.wait_recv()

    pass_on(0, 0)
    pass_on(1, 0)
    pass_on(0, 1)
    arrived(0, 1)
    point_terms(0, across, True)
    pass_on(0, 2)
    point_terms(0, middle, False)
    arrived(1, 1)
    point_terms(1, across, True)
    pass_on(1, 1)
    arrived(0, 0)
    arrived(0, 2)
    point_last(0, sides)
    pass_on(1, 2)
    ya0 = chip_sums(0)
    point_terms(1, middle, False)
    arrived(1, 0)
    arrived(1, 2)
    point_last(1, sides)
    ya1 = chip_sums(1)
    input_terms(0)
    za0, yb0 = second(0, ya0)
    input_terms(1)
    ig_out = pltpu.make_async_copy(ig_ref, ig_hbm.at[0], out_sem)
    ig_out.start()

    za1, yb1 = second(1, ya1)
    x_copies = [third(0, za0, yb0)]
    x_copies.append(third(1, za1, yb1))
    width = pg_ref.shape[1]
    pick = lax.broadcasted_iota(jnp.int32, (width, zc), 1) == (
        member * width + lax.broadcasted_iota(jnp.int32, (width, zc), 0)
    )
    pick = pick.astype(F32)
    for b in (0, 1):
        sums = [v_ref[b].astype(F32), None]
        for k, copy in x_copies[b]:
            copy.wait_recv()
            part = rx_ref[b, k].astype(F32)
            sums[k % 2] = part if sums[k % 2] is None else sums[k % 2] + part
        low = jnp.where(core == 0, sums[0], sums[1])
        high = jnp.where(core == 0, sums[1], sums[0])
        block = jnp.concatenate([low, high], axis=0)
        pg_ref[b] = scale * lax.dot_general(
            pick, block, NT, preferred_element_type=F32, precision=lax.Precision.HIGHEST
        )
    ig_out.wait()
    for copy in started:
        copy.wait_send()

    def finish(k, carry):
        for b in (0, 1):
            core_copy(b, k).wait_send()
        return carry

    lax.fori_loop(0, nz, finish, 0)

    def finish_z(k, carry):
        for b in (0, 1):
            zb_copy(b, k).wait_send()
        return carry

    lax.fori_loop(1, nz, finish_z, 0)


def shards(features, depthwise_kernels, point_weights, proj_weight, class_weight, labels):
    rows, cols, channels = features.shape[1:]
    outc = point_weights.shape[2]
    ndp, nrow, nlon = (lax.axis_size(a) for a in ("dp", "row", "lon"))
    nz = nrow // 2
    hops = (DILATION_INNER // rows, DILATION_OUTER // rows)
    groups = cols // GROUP
    gp = -(-rows * GROUP // 16) * 16
    pix = groups * gp
    pix_pad = -(-pix // 128) * 128
    pitch = -(-cols // 16) * 16
    zc = channels // nz
    hc = zc // 2
    half = outc // ndp // 2
    chunk = channels // (nrow * nlon)
    scale = 1.0 / math.sqrt(ndp * nrow * nlon * rows * cols)

    vmem = pl.BlockSpec(memory_space=pltpu.VMEM)
    hbm = pl.BlockSpec(memory_space=pl.ANY)
    kernels = depthwise_kernels.transpose(1, 2, 0, 3)
    classes = class_weight.T
    label_rows = labels.transpose(1, 0, 2)
    dma = lambda n: pltpu.SemaphoreType.DMA((n,))
    scratch = [
        pltpu.VMEM(features.shape[1:], BF16),
        pltpu.VMEM(kernels.shape, BF16),
        pltpu.VMEM(point_weights.shape, BF16),
        pltpu.VMEM(proj_weight.shape, BF16),
        pltpu.VMEM(classes.shape, BF16),
        pltpu.VMEM(label_rows.shape, jnp.int32),
        pltpu.VMEM(features.shape[1:], BF16),
        dma(7), pltpu.SemaphoreType.DMA,
        pltpu.VMEM((rows, pitch, channels), BF16),
        pltpu.VMEM((pix_pad, channels), BF16),
        pltpu.VMEM((rows * pitch, pix_pad), BF16),
        pltpu.VMEM((128, 128), F32),
        pltpu.VMEM((pix, 128), F32),
        pltpu.VMEM((128, outc), BF16),
        pltpu.VMEM((18, channels), F32),
        pltpu.VMEM((18, 16, channels), BF16),
        pltpu.VMEM((6, pix, outc), F32),
        pltpu.VMEM((3, 2, pix, outc), BF16),
        pltpu.VMEM((3, 2, pix, outc), BF16),
        pltpu.VMEM((3, 2, gp, outc), BF16),
        pltpu.VMEM((3, 2, gp, outc), BF16),
        pltpu.VMEM((4, pix, outc), BF16),
        pltpu.VMEM((4, pix, outc), BF16),
        pltpu.VMEM((3, 5, gp, outc), BF16),
        pltpu.VMEM((3, 9, gp, outc), BF16),
        pltpu.VMEM((9, outc, pix_pad), BF16),
        pltpu.VMEM((pix, channels), F32),
        pltpu.VMEM((2, outc, channels), F32),
        pltpu.VMEM((2, nz, 2, ndp, half, zc), BF16),
        pltpu.VMEM((2, nz, ndp, half, zc), BF16),
        pltpu.VMEM((2, ndp, nz, half, hc), BF16),
        pltpu.VMEM((2, nz, ndp, half, hc), BF16),
        pltpu.VMEM((2, ndp, nz, half, hc), BF16),
        pltpu.VMEM((2, nz, ndp, half, hc), BF16),
        pltpu.VMEM((2, nz, half, hc), BF16),
        pltpu.VMEM((2, ndp, half, hc), BF16),
        pltpu.VMEM((2, nz, half, hc), BF16),
        pltpu.VMEM((2, ndp, half, hc), BF16),
        pltpu.VMEM((2, half, zc), BF16),
        pltpu.VMEM((2, 2 * nlon, half, zc), BF16),
        dma(24), dma(24), dma(12), dma(12), dma(12), dma(12), dma(24), dma(24),
        dma(2 * nz), dma(2 * nz), dma(4 * ndp), dma(4 * ndp), dma(2 * nz), dma(2 * nz),
        dma(2 * nz), dma(2 * nz), dma(2 * ndp), dma(2 * ndp), dma(4 * nlon), dma(4 * nlon),
    ]
    return pl.pallas_call(
        functools.partial(kernel, (ndp, nrow, nlon), hops, scale),
        out_shape=(
            jax.ShapeDtypeStruct(features.shape, BF16),
            jax.ShapeDtypeStruct((2, chunk, outc // ndp), F32),
        ),
        in_specs=[hbm] * 6,
        out_specs=(hbm, vmem),
        scratch_shapes=scratch,
        compiler_params=pltpu.CompilerParams(
            collective_id=0, has_side_effects=True, vmem_limit_bytes=56 * 1024 * 1024
        ),
        cost_estimate=pl.CostEstimate(
            flops=54 * 2 * pix * channels * outc, bytes_accessed=8 * pix * channels, transcendentals=0
        ),
    )(features, kernels, point_weights, proj_weight, classes, label_rows)


def solution(mesh):
    placed = (P("dp", "row", "lon", None), P(), P(), P(), P(), P("dp", "row", "lon"))
    return jax.shard_map(
        shards,
        mesh=mesh,
        in_specs=placed,
        out_specs=(P("dp", "row", "lon", None), P(None, ("row", "lon"), "dp")),
        check_vma=False,
    )
```
